32 devices in a mesh: replica: 2 (over x), node: 2 (over core), dev: 8 (over z, y).
Axes of the slice: x: 2, y: 2, z: 4, core: 2. Of those that a mesh axis runs over, the one named last changes fastest.
Arguments:
- tokens: bfloat16 [64, 7168], P(('replica', 'node', 'dev')), parts along dimension 0, may hold values from -6 to 6
- routes: int32 [64, 1], P(('replica', 'node', 'dev')), parts along dimension 0, may hold values from 0 to 1; in each aligned block of 2 rows (0 to 1, 2 to 3, ...) at most 2 rows name the same one
- route_weights: bfloat16 [64, 1], P(('replica', 'node', 'dev')), parts along dimension 0, may hold values from 0.049804688 to 1
- gate_weight: bfloat16 [16, 7168, 256], P(('node', 'dev')), may hold values from -0.0625 to 0.0625
- up_weight: bfloat16 [16, 7168, 256], P(('node', 'dev')), may hold values from -0.0625 to 0.0625
- down_weight: bfloat16 [16, 256, 7168], P(('node', 'dev')), may hold values from -0.125 to 0.125
Outputs:
- mixed: bfloat16 [64, 7168], P(('replica', 'node', 'dev')), parts along dimension 0
The draws below stay inside these ranges and needn't reach their ends.
There are 2 independent parts, one for each index of `replica`. The reference program is written for one: setup_inputs(seed, part) draws one part's arguments, and reference() takes and returns one part's arrays. A program takes and returns all parts, laid end to end along the dimension named above; an argument that names none is the same for every part. Nothing has to cross between parts.
Inputs may be any that keep to these rules, and one draw needn't show every extreme that they name: `routes`: each row names 1 expert; among the rows of one device no expert is named by more than 2 rows, and in every draw some expert is named by exactly 2 rows of some device.
All inputs are finite; a program needn't handle non-finite values.
Results may differ from the reference program's by a relative error of at most 0.0049.
Values may be sent and summed in bfloat16 or wider, within the bound.
No kernel may reach another device: no remote copies, remote signals or barrier semaphores. Data moves between devices by JAX's collectives and lax.ppermute only.
A program may use at most 128 MiB of HBM per device.

```python
import math
import jax
import jax.numpy as jnp
import numpy as np
from jax import lax

D = 7168
FF = 2048
TOK_DEV = 2
SPLIT = 8
HS = 256
EXPERTS = 2
TOP = 1
CAP = 2
TOKENS = 32


def block_levels(stream_key, shape, pieces, smallest, high):
    loudness = 1.0
    for dim, shards_of in pieces:
        steps = jax.random.uniform(jax.random.fold_in(jax.random.fold_in(stream_key, 6), dim), (shards_of,), jnp.float32, smallest / len(pieces), high / len(pieces))
        loudness = loudness * jnp.repeat(jnp.exp(steps), shape[dim] // shards_of).reshape((-1,) + (1,) * (len(shape) - 1 - dim))
    return loudness


def routed_block(rng, own, number, rows, number_of, top, limit, slope):
    order = jax.random.permutation(rng, number_of)
    heavy_load, usual = load_shares(number_of, rows * top, limit, slope, True), load_shares(number_of, rows * top, limit, slope, False)
    places = jnp.arange(number_of)

    def named(tallies, rotation):
        used = int((tallies > 0).sum())
        fixed = max(1, used // 4)
        moved = fixed + (places - fixed + rotation * (used - fixed)) % max(1, number_of - fixed)
        return jnp.zeros((number_of,), jnp.int32).at[order[jnp.where(places < fixed, places, moved)]].set(jnp.asarray(tallies, jnp.int32))

    tallies = jnp.where(number % 4 == 0, named(heavy_load, number // 4), named(usual, number - number // 4 - 1))
    mixed = jax.random.permutation(jax.random.fold_in(own, 3), number_of)
    source_of, receiver = mixed[0:number_of // 2 * 2:2], mixed[1:number_of // 2 * 2:2]
    margin = jnp.minimum(tallies[source_of] - 1, limit - tallies[receiver]) // 2
    margin = jnp.where((source_of == order[0]) | (receiver == order[0]) | (tallies[receiver] == 0), 0, jnp.maximum(margin, 0))
    moved = jax.random.randint(jax.random.fold_in(own, 4), (number_of // 2,), 0, 1 << 20) % (margin + 1)
    tallies = tallies.at[source_of].add(-moved).at[receiver].add(moved)
    labels = jnp.searchsorted(jnp.cumsum(tallies), jnp.arange(rows * top), side="right").astype(jnp.int32)
    table = labels.reshape(top, rows).T
    table = table[jax.random.permutation(jax.random.fold_in(own, 1), rows)]
    rotation = jax.random.randint(jax.random.fold_in(own, 2), (rows, 1), 0, top)
    return jnp.take_along_axis(table, (jnp.arange(top)[None, :] + rotation) % top, axis=1)


def load_shares(count, total, reach, skew, full):
    loads = [(1 << 20) // math.isqrt(standing ** skew) + 1 for standing in range(1, count + 1)]
    largest = reach if full else min(reach, max(-(-total // count), total * loads[0] // sum(loads)))
    least = 1 if total - largest >= count - 1 else 0
    holding, spare = [largest] + [least] * (count - 1), total - largest - least * (count - 1)
    while spare > 0:
        free = [i for i in range(1, count) if holding[i] < largest] or [i for i in range(1, count) if holding[i] < reach]
        whole, budget = sum([loads[i] for i in free]), spare
        for i in free:
            more = min(reach - holding[i], max(1, budget * loads[i] // whole), spare)
            holding[i] = holding[i] + more
            spare = spare - more
    return np.array(holding)


def scatter_about(own_key, shape, spread, limit, shards=(), kind=jnp.bfloat16):
    drawn = spread * jax.random.normal(own_key, shape, jnp.float32)
    if shards:
        drawn = drawn * block_levels(own_key, shape, shards, -0.22, 0.18)
    return jnp.clip(drawn, -limit, limit).astype(kind)


def setup_inputs(seed: int = 0, part: int = 0) -> dict:
    streams_of = jax.random.split(jax.random.key(seed), 7)
    own_keys = jax.random.split(jax.random.fold_in(streams_of[6], part), 7)
    tokens = scatter_about(own_keys[0], (TOKENS, D), 1.0, 6.0, ((0, 16),))
    routes_keys = jax.random.split(jax.random.fold_in(own_keys[1], 1), TOKENS // TOK_DEV)
    routes_turns = jax.random.permutation(jax.random.fold_in(own_keys[1], 3), TOKENS // TOK_DEV)
    routes = jax.vmap(lambda own, number: routed_block(jax.random.fold_in(own_keys[1], 2), own, number, TOK_DEV, EXPERTS, TOP, CAP, 2))(routes_keys, routes_turns).reshape((TOKENS, TOP))
    route_weights = jnp.clip(jnp.exp(math.log(1.0) - 2.9996462 * jax.random.uniform(own_keys[2], (TOKENS, TOP), jnp.float32) ** block_levels(own_keys[2], (TOKENS, TOP), ((0, 16),), -0.2, 0.2)), 0.049804688, 1.0).astype(jnp.bfloat16)
    gate_weight = scatter_about(streams_of[3], (EXPERTS * SPLIT, D, HS), D ** -0.5, 0.0625, ((0, 16),))
    up_weight = scatter_about(streams_of[4], (EXPERTS * SPLIT, D, HS), D ** -0.5, 0.0625, ((0, 16),))
    down_weight = scatter_about(streams_of[5], (EXPERTS * SPLIT, HS, D), FF ** -0.5, 0.125, ((0, 16),))
    return dict(tokens=tokens, routes=routes, route_weights=route_weights, gate_weight=gate_weight, up_weight=up_weight, down_weight=down_weight)


def reference(tokens, routes, route_weights, gate_weight, up_weight, down_weight):
    rows32 = tokens.astype(jnp.float32)
    weights32 = route_weights.astype(jnp.float32)
    gate_split = gate_weight.reshape(EXPERTS, SPLIT, D, HS)
    up_split = up_weight.reshape(EXPERTS, SPLIT, D, HS)
    down_split = down_weight.reshape(EXPERTS, SPLIT * HS, D)

    def add_expert(total, index):
        gate_full = jnp.transpose(gate_split[index], (1, 0, 2)).reshape(D, FF).astype(jnp.float32)
        up_full = jnp.transpose(up_split[index], (1, 0, 2)).reshape(D, FF).astype(jnp.float32)
        gate = jnp.dot(rows32, gate_full, precision=lax.Precision.HIGHEST)
        upper = jnp.dot(rows32, up_full, precision=lax.Precision.HIGHEST)
        hidden = (jax.nn.silu(gate) * upper).astype(jnp.bfloat16)
        output = jnp.dot(hidden.astype(jnp.float32), down_split[index].astype(jnp.float32), precision=lax.Precision.HIGHEST)
        column = jnp.sum(jnp.where(routes == index, weights32, jnp.float32(0.0)), axis=1)
        return total + output * column[:, None], None

    start = jnp.zeros((TOKENS, D), jnp.float32)
    total, unused = lax.scan(add_expert, start, jnp.arange(EXPERTS, dtype=jnp.int32))
    return total.astype(jnp.bfloat16)
```

```python
import functools

import jax
import jax.numpy as jnp
from jax import lax
from jax.experimental import pallas as pl
from jax.experimental.pallas import tpu as pltpu
from jax.sharding import PartitionSpec as P

SPLIT = 8
LANES = 128
VMEM_LIMIT = 48 * 1024 * 1024


def pack_kernel(tokens_ref, routes_ref, weights_ref, packed_ref):
    rows, width = tokens_ref.shape
    copies = packed_ref.shape[0]
    extra = packed_ref.shape[2] - width
    columns = lax.broadcasted_iota(jnp.int32, (rows, extra), 1)
    combine = jnp.zeros((rows, extra), jnp.float32)
    for k in range(routes_ref.shape[1]):
        chosen = columns == routes_ref[:, k : k + 1]
        combine += jnp.where(chosen, weights_ref[:, k : k + 1].astype(jnp.float32), 0.0)
    combine = combine.astype(jnp.bfloat16)
    for c in range(copies):
        packed_ref[c, :, :width] = tokens_ref[...]
        packed_ref[c, :, width:] = combine


def expert_kernel(
    expert_ref, own_ref, other_ref, gate_hbm, up_hbm, down_hbm, own_out, other_out,
    gate_buf, up_buf, down_buf, gate_sem, up_sem, down_sem,
):
    rows = own_ref.shape[0]
    width, hidden_units = gate_buf.shape
    steps = gate_sem.shape[0]
    tall = width // steps

    def gate_copy(i):
        part = pl.ds(i * tall, tall)
        return pltpu.make_async_copy(gate_hbm.at[0, part], gate_buf.at[part], gate_sem.at[i])

    def up_copy(i):
        part = pl.ds(i * tall, tall)
        return pltpu.make_async_copy(up_hbm.at[0, part], up_buf.at[part], up_sem.at[i])

    def down_copy(i):
        part = pl.ds(i * tall, tall)
        return pltpu.make_async_copy(
            down_hbm.at[0, :, part], down_buf.at[:, part], down_sem.at[i]
        )

    for i in range(steps):
        gate_copy(i).start()
        up_copy(i).start()
    for i in range(steps):
        down_copy(i).start()

    combine = jnp.concatenate([own_ref[:, width:], other_ref[:, width:]], axis=0)
    columns = lax.broadcasted_iota(jnp.int32, combine.shape, 1)
    scale = jnp.sum(
        jnp.where(columns == expert_ref[0], combine.astype(jnp.float32), 0.0),
        axis=1, keepdims=True,
    )
    gate = jnp.zeros((2 * rows, hidden_units), jnp.float32)
    upper = jnp.zeros((2 * rows, hidden_units), jnp.float32)
    for i in range(steps):
        part = slice(i * tall, (i + 1) * tall)
        block = jnp.concatenate([own_ref[:, part], other_ref[:, part]], axis=0)
        gate_copy(i).wait()
        gate += jnp.dot(block, gate_buf[part, :], preferred_element_type=jnp.float32)
        up_copy(i).wait()
        upper += jnp.dot(block, up_buf[part, :], preferred_element_type=jnp.float32)
    hidden = (gate / (1.0 + jnp.exp(-gate)) * upper).astype(jnp.bfloat16)
    for i in range(steps):
        part = slice(i * tall, (i + 1) * tall)
        down_copy(i).wait()
        output = scale * jnp.dot(
            hidden, down_buf[:, part], preferred_element_type=jnp.float32
        )
        own_out[:, part] = output[:rows].astype(own_out.dtype)
        other_out[:, part] = output[rows:].astype(other_out.dtype)


def per_device(tokens, routes, route_weights, gate_weight, up_weight, down_weight):
    tok_rows, width = tokens.shape
    hidden_units = gate_weight.shape[2]
    nodes = lax.axis_size("node")
    devs = lax.axis_size("dev")
    per_node = devs // SPLIT
    experts = nodes * per_node
    wide = width + -(-experts // LANES) * LANES
    rows = devs * tok_rows
    vmem = pl.BlockSpec(memory_space=pltpu.VMEM)
    anywhere = pl.BlockSpec(memory_space=pl.ANY)
    swap = [(i, i ^ 1) for i in range(nodes)]

    packed = pl.pallas_call(
        pack_kernel,
        out_shape=jax.ShapeDtypeStruct((devs, tok_rows, wide), jnp.bfloat16),
        in_specs=[vmem] * 3,
        out_specs=vmem,
        name="pack",
    )(tokens, routes, route_weights)
    own = lax.all_to_all(packed, "dev", split_axis=0, concat_axis=0, tiled=True)
    own = own.reshape(rows, wide)
    other = lax.ppermute(own, "node", swap)

    expert = lax.axis_index("node") * per_node + lax.axis_index("dev") // SPLIT
    steps = 7
    own_out, other_out = pl.pallas_call(
        expert_kernel,
        out_shape=(
            jax.ShapeDtypeStruct((rows, width), jnp.float32),
            jax.ShapeDtypeStruct((rows, width), jnp.bfloat16),
        ),
        in_specs=[pl.BlockSpec(memory_space=pltpu.SMEM), vmem, vmem] + [anywhere] * 3,
        out_specs=(vmem, vmem),
        scratch_shapes=[
            pltpu.VMEM((width, hidden_units), jnp.bfloat16),
            pltpu.VMEM((width, hidden_units), jnp.bfloat16),
            pltpu.VMEM((hidden_units, width), jnp.bfloat16),
            pltpu.SemaphoreType.DMA((steps,)),
            pltpu.SemaphoreType.DMA((steps,)),
            pltpu.SemaphoreType.DMA((steps,)),
        ],
        compiler_params=pltpu.CompilerParams(vmem_limit_bytes=VMEM_LIMIT),
        name="expert",
    )(expert.reshape(1).astype(jnp.int32), own, other, gate_weight, up_weight, down_weight)
    arrived = lax.ppermute(other_out, "node", swap)
    partial = (own_out + arrived.astype(jnp.float32)).astype(jnp.bfloat16)
    returned = lax.all_to_all(
        partial.reshape(devs, tok_rows, width), "dev", split_axis=0, concat_axis=0, tiled=True
    )
    return jnp.sum(returned.astype(jnp.float32), axis=0).astype(jnp.bfloat16)


def solution(mesh):
    rows = P(("replica", "node", "dev"), None)
    shards = P(("node", "dev"), None, None)
    return jax.shard_map(
        per_device,
        mesh=mesh,
        in_specs=(rows, rows, rows, shards, shards, shards),
        out_specs=rows,
        check_vma=False,
    )
```

```python
import jax
import jax.numpy as jnp
from jax import lax
from jax.experimental import pallas as pl
from jax.experimental.pallas import tpu as pltpu
from jax.sharding import PartitionSpec as P

SPLIT = 8
LANES = 128
LOAD_LIMIT = 48 * 1024 * 1024
HEAD = 5632
DOWN_STEP = 1792
COLUMNS = 512


def pack_kernel(tokens_ref, routes_ref, weights_ref, packed_ref):
    rows, width = tokens_ref.shape
    copies = packed_ref.shape[0]
    extra = packed_ref.shape[2] - width
    columns = lax.broadcasted_iota(jnp.int32, (rows, extra), 1)
    combine = jnp.zeros((rows, extra), jnp.float32)
    for k in range(routes_ref.shape[0]):
        route = jnp.concatenate([routes_ref[k : k + 1, r : r + 1] for r in range(rows)], axis=0)
        weight = weights_ref[:, k : k + 1].astype(jnp.float32)
        combine += jnp.where(columns == route, weight, 0.0)
    combine = combine.astype(jnp.bfloat16)
    for c in range(copies):
        packed_ref[c, :, :width] = tokens_ref[...]
        packed_ref[c, :, width:] = combine


def load_kernel(weight_hbm, part_ref, sem):
    head = pl.ds(0, part_ref.shape[0])
    copy = pltpu.make_async_copy(weight_hbm.at[0, head], part_ref, sem)
    copy.start()
    copy.wait()


def expert_kernel(
    own_ref, other_ref, gate_head, up_head, gate_hbm, up_hbm, down_hbm, own_out, other_out,
    gate_tail, up_tail, down_buf, gate_sem, up_sem, down_sem,
):
    rows = own_ref.shape[0]
    head, hidden_units = gate_head.shape
    width = own_out.shape[1]
    rest = pl.ds(head, width - head)
    gate_copy = pltpu.make_async_copy(gate_hbm.at[0, rest], gate_tail, gate_sem)
    up_copy = pltpu.make_async_copy(up_hbm.at[0, rest], up_tail, up_sem)

    def down_copy(i):
        part = pl.ds(i * DOWN_STEP, DOWN_STEP)
        return pltpu.make_async_copy(
            down_hbm.at[0, :, part], down_buf.at[:, part], down_sem.at[i]
        )

    gate_copy.start()
    up_copy.start()
    for i in range(width // DOWN_STEP):
        down_copy(i).start()

    expert = lax.axis_index("node") * (lax.axis_size("dev") // SPLIT) + lax.axis_index("dev") // SPLIT
    combine = jnp.concatenate([own_ref[:, width:], other_ref[:, width:]], axis=0)
    columns = lax.broadcasted_iota(jnp.int32, combine.shape, 1)
    scale = jnp.sum(
        jnp.where(columns == expert, combine.astype(jnp.float32), 0.0), axis=1, keepdims=True
    )
    gate = jnp.zeros((2 * rows, hidden_units), jnp.float32)
    upper = jnp.zeros((2 * rows, hidden_units), jnp.float32)
    for start in range(0, head, COLUMNS):
        part = slice(start, start + COLUMNS)
        block = jnp.concatenate([own_ref[:, part], other_ref[:, part]], axis=0)
        gate += jnp.dot(block, gate_head[part, :], preferred_element_type=jnp.float32)
        upper += jnp.dot(block, up_head[part, :], preferred_element_type=jnp.float32)
    block = jnp.concatenate([own_ref[:, head:width], other_ref[:, head:width]], axis=0)
    gate_copy.wait()
    gate += jnp.dot(block, gate_tail[...], preferred_element_type=jnp.float32)
    up_copy.wait()
    upper += jnp.dot(block, up_tail[...], preferred_element_type=jnp.float32)
    hidden = (gate / (1.0 + jnp.exp(-gate)) * upper).astype(jnp.bfloat16)
    for i in range(width // DOWN_STEP):
        part = slice(i * DOWN_STEP, (i + 1) * DOWN_STEP)
        down_copy(i).wait()
        output = scale * jnp.dot(
            hidden, down_buf[:, part], preferred_element_type=jnp.float32
        )
        own_out[:, part] = output[:rows].astype(own_out.dtype)
        other_out[:, part] = output[rows:].astype(other_out.dtype)


def load_head(weight):
    part = (HEAD, weight.shape[2])
    return pl.pallas_call(
        load_kernel,
        out_shape=pltpu.VMEM(part, weight.dtype),
        in_specs=[pl.BlockSpec(memory_space=pltpu.HBM)],
        out_specs=pl.BlockSpec(memory_space=pltpu.VMEM),
        scratch_shapes=[pltpu.SemaphoreType.DMA],
        compiler_params=pltpu.CompilerParams(vmem_limit_bytes=LOAD_LIMIT),
        cost_estimate=pl.CostEstimate(
            flops=0, transcendentals=0, bytes_accessed=2 * part[0] * part[1]
        ),
        name="load",
    )(weight)


def per_device(tokens, routes, route_weights, gate_weight, up_weight, down_weight):
    tok_rows, width = tokens.shape
    hidden_units = gate_weight.shape[2]
    nodes = lax.axis_size("node")
    devs = lax.axis_size("dev")
    per_node = devs // SPLIT
    experts = nodes * per_node
    wide = width + -(-experts // LANES) * LANES
    rows = devs * tok_rows
    vmem = pl.BlockSpec(memory_space=pltpu.VMEM)
    swap = [(i, i ^ 1) for i in range(nodes)]

    packed = pl.pallas_call(
        pack_kernel,
        out_shape=jax.ShapeDtypeStruct((devs, tok_rows, wide), jnp.bfloat16),
        in_specs=[vmem] * 3,
        out_specs=vmem,
        name="pack",
    )(tokens, routes.T, route_weights)
    own = lax.all_to_all(packed, "dev", split_axis=0, concat_axis=0, tiled=True)
    gate_head = load_head(gate_weight)
    own, gate_head = lax.optimization_barrier((own, gate_head))
    own = own.reshape(rows, wide)
    own, up_source = lax.optimization_barrier((own, up_weight))
    other = lax.ppermute(own, "node", swap)
    up_head = load_head(up_source)
    other, up_head = lax.optimization_barrier((other, up_head))
    tail = (width - HEAD, hidden_units)
    resident = 2 * (2 * rows * wide + 2 * HEAD * hidden_units) + 6 * rows * width
    own_out, other_out = pl.pallas_call(
        expert_kernel,
        out_shape=(
            jax.ShapeDtypeStruct((rows, width), jnp.float32),
            jax.ShapeDtypeStruct((rows, width), jnp.bfloat16),
        ),
        in_specs=[vmem] * 4 + [pl.BlockSpec(memory_space=pltpu.HBM)] * 3,
        out_specs=(vmem, vmem),
        scratch_shapes=[
            pltpu.VMEM(tail, jnp.bfloat16),
            pltpu.VMEM(tail, jnp.bfloat16),
            pltpu.VMEM((hidden_units, width), jnp.bfloat16),
            pltpu.SemaphoreType.DMA,
            pltpu.SemaphoreType.DMA,
            pltpu.SemaphoreType.DMA((width // DOWN_STEP,)),
        ],
        compiler_params=pltpu.CompilerParams(
            vmem_limit_bytes=52 * 1024 * 1024 - resident
        ),
        name="expert",
    )(own, other, gate_head, up_head, gate_weight, up_weight, down_weight)
    arrived = lax.ppermute(other_out, "node", swap)
    partial = (own_out + arrived.astype(jnp.float32)).astype(jnp.bfloat16)
    returned = lax.all_to_all(
        partial.reshape(devs, tok_rows, width), "dev", split_axis=0, concat_axis=0, tiled=True
    )
    return jnp.sum(returned.astype(jnp.float32), axis=0).astype(jnp.bfloat16)


def solution(mesh):
    rows = P(("replica", "node", "dev"), None)
    shards = P(("node", "dev"), None, None)
    return jax.shard_map(
        per_device,
        mesh=mesh,
        in_specs=(rows, rows, rows, shards, shards, shards),
        out_specs=rows,
        check_vma=False,
    )
```

```python
import jax
import jax.numpy as jnp
from jax import lax
from jax.experimental import pallas as pl
from jax.experimental.pallas import tpu as pltpu
from jax.sharding import PartitionSpec as P

SPLIT = 8
LANES = 128
VMEM_LIMIT = 32 * 1024 * 1024
COLUMNS = 1024


def pack_kernel(tokens_ref, routes_ref, weights_ref, packed_ref):
    rows, width = tokens_ref.shape
    copies = packed_ref.shape[0]
    extra = packed_ref.shape[2] - width
    columns = lax.broadcasted_iota(jnp.int32, (rows, extra), 1)
    combine = jnp.zeros((rows, extra), jnp.float32)
    for k in range(routes_ref.shape[0]):
        route = jnp.concatenate([routes_ref[k : k + 1, r : r + 1] for r in range(rows)], axis=0)
        weight = weights_ref[:, k : k + 1].astype(jnp.float32)
        combine += jnp.where(columns == route, weight, 0.0)
    combine = combine.astype(jnp.bfloat16)
    for c in range(copies):
        packed_ref[c, :, :width] = tokens_ref[...]
        packed_ref[c, :, width:] = combine


def expert_kernel(own_ref, other_ref, gate_ref, up_ref, down_ref, own_out, other_out):
    devs, tok_rows, wide = own_ref.shape
    _, width, hidden_units = gate_ref.shape
    rows = devs * tok_rows

    def tokens_part(part):
        halves = [ref[:, :, part] for ref in (own_ref, other_ref)]
        return jnp.concatenate([half.reshape(rows, half.shape[2]) for half in halves], axis=0)

    expert = lax.axis_index("node") * (lax.axis_size("dev") // SPLIT) + lax.axis_index("dev") // SPLIT
    combine = tokens_part(slice(width, wide)).astype(jnp.float32)
    columns = lax.broadcasted_iota(jnp.int32, combine.shape, 1)
    scale = jnp.sum(jnp.where(columns == expert, combine, 0.0), axis=1, keepdims=True)
    gate = jnp.zeros((2 * rows, hidden_units), jnp.float32)
    upper = jnp.zeros((2 * rows, hidden_units), jnp.float32)
    for start in range(0, width, COLUMNS):
        part = slice(start, start + COLUMNS)
        block = tokens_part(part)
        gate += jnp.dot(block, gate_ref[0, part, :], preferred_element_type=jnp.float32)
        upper += jnp.dot(block, up_ref[0, part, :], preferred_element_type=jnp.float32)
    hidden = (gate / (1.0 + jnp.exp(-gate)) * upper).astype(jnp.bfloat16)
    for start in range(0, width, COLUMNS):
        part = slice(start, start + COLUMNS)
        output = scale * jnp.dot(
            hidden, down_ref[0, :, part], preferred_element_type=jnp.float32
        )
        own_out[:, :, part] = output[:rows].reshape(devs, tok_rows, COLUMNS)
        other = output[rows:].astype(jnp.bfloat16)
        other_out[:, :, part] = other.reshape(devs, tok_rows, COLUMNS)


def per_device(tokens, routes, route_weights, gate_weight, up_weight, down_weight):
    tok_rows, width = tokens.shape
    nodes = lax.axis_size("node")
    devs = lax.axis_size("dev")
    per_node = devs // SPLIT
    experts = nodes * per_node
    wide = width + -(-experts // LANES) * LANES
    vmem = pl.BlockSpec(memory_space=pltpu.VMEM)
    swap = [(i, i ^ 1) for i in range(nodes)]

    packed = pl.pallas_call(
        pack_kernel,
        out_shape=jax.ShapeDtypeStruct((devs, tok_rows, wide), jnp.bfloat16),
        in_specs=[vmem] * 3,
        out_specs=vmem,
        name="pack",
    )(tokens, routes.T, route_weights)
    here = [(i, i) for i in range(nodes)]
    packed, *weights = lax.optimization_barrier((packed, gate_weight, up_weight, down_weight))
    resident = [lax.ppermute(weight, "node", here) for weight in weights]
    own = lax.all_to_all(packed, "dev", split_axis=0, concat_axis=0, tiled=True)
    other = lax.ppermute(own, "node", swap)
    own_out, other_out = pl.pallas_call(
        expert_kernel,
        out_shape=(
            jax.ShapeDtypeStruct((devs, tok_rows, width), jnp.float32),
            jax.ShapeDtypeStruct((devs, tok_rows, width), jnp.bfloat16),
        ),
        in_specs=[vmem] * 5,
        out_specs=(vmem, vmem),
        compiler_params=pltpu.CompilerParams(vmem_limit_bytes=VMEM_LIMIT),
        name="expert",
    )(own, other, *resident)
    arrived = lax.ppermute(other_out, "node", swap)
    partial = (own_out + arrived.astype(jnp.float32)).astype(jnp.bfloat16)
    returned = lax.all_to_all(
        partial, "dev", split_axis=0, concat_axis=0, tiled=True
    )
    return jnp.sum(returned.astype(jnp.float32), axis=0).astype(jnp.bfloat16)


def solution(mesh):
    rows = P(("replica", "node", "dev"), None)
    shards = P(("node", "dev"), None, None)
    return jax.shard_map(
        per_device,
        mesh=mesh,
        in_specs=(rows, rows, rows, shards, shards, shards),
        out_specs=rows,
        check_vma=False,
    )
```

```python
import jax
import jax.numpy as jnp
from jax import lax
from jax.experimental import pallas as pl
from jax.experimental.pallas import tpu as pltpu
from jax.sharding import PartitionSpec as P

SPLIT = 8
LANES = 128
VMEM_ROOM = 52 * 1024 * 1024
EXPERT_LIMIT = 24 * 1024 * 1024
COLUMNS = 1024


def pack_kernel(tokens_ref, routes_ref, weights_ref, packed_ref):
    rows, width = tokens_ref.shape
    copies = packed_ref.shape[0]
    extra = packed_ref.shape[2] - width
    columns = lax.broadcasted_iota(jnp.int32, (rows, extra), 1)
    combine = jnp.zeros((rows, extra), jnp.float32)
    for k in range(routes_ref.shape[0]):
        route = jnp.concatenate([routes_ref[k : k + 1, r : r + 1] for r in range(rows)], axis=0)
        weight = weights_ref[:, k : k + 1].astype(jnp.float32)
        combine += jnp.where(columns == route, weight, 0.0)
    combine = combine.astype(jnp.bfloat16)
    for c in range(copies):
        packed_ref[c, :, :width] = tokens_ref[...]
        packed_ref[c, :, width:] = combine


def load_kernel(weight_hbm, held_ref, sem):
    copy = pltpu.make_async_copy(weight_hbm, held_ref, sem)
    copy.start()
    copy.wait()


def load(weight, held):
    return pl.pallas_call(
        load_kernel,
        out_shape=pltpu.VMEM(weight.shape, weight.dtype),
        in_specs=[pl.BlockSpec(memory_space=pltpu.HBM)],
        out_specs=pl.BlockSpec(memory_space=pltpu.VMEM),
        scratch_shapes=[pltpu.SemaphoreType.DMA],
        compiler_params=pltpu.CompilerParams(vmem_limit_bytes=VMEM_ROOM - held),
        cost_estimate=pl.CostEstimate(
            flops=0, transcendentals=0, bytes_accessed=2 * weight.size
        ),
        name="load",
    )(weight)


def expert_kernel(
    near_ref, far_ref, near_other_ref, far_other_ref, gate_ref, up_ref, down_ref,
    own_out, other_out,
):
    groups, tok_rows, wide = near_ref.shape
    _, width, hidden_units = gate_ref.shape
    rows = groups * tok_rows
    refs = (near_ref, far_ref, near_other_ref, far_other_ref)

    def tokens_part(part):
        pieces = [ref[:, :, part] for ref in refs]
        return jnp.concatenate([piece.reshape(rows, piece.shape[2]) for piece in pieces], axis=0)

    dev = lax.axis_index("dev")
    expert = lax.axis_index("node") * (lax.axis_size("dev") // SPLIT) + dev // SPLIT
    side = dev % 2
    combine = tokens_part(slice(width, wide)).astype(jnp.float32)
    columns = lax.broadcasted_iota(jnp.int32, combine.shape, 1)
    scale = jnp.sum(jnp.where(columns == expert, combine, 0.0), axis=1, keepdims=True)
    gate = jnp.zeros((4 * rows, hidden_units), jnp.float32)
    upper = jnp.zeros((4 * rows, hidden_units), jnp.float32)
    for start in range(0, width, COLUMNS):
        part = slice(start, start + COLUMNS)
        block = tokens_part(part)
        gate += jnp.dot(block, gate_ref[0, part, :], preferred_element_type=jnp.float32)
        upper += jnp.dot(block, up_ref[0, part, :], preferred_element_type=jnp.float32)
    hidden = (gate / (1.0 + jnp.exp(-gate)) * upper).astype(jnp.bfloat16)
    for start in range(0, width, COLUMNS):
        part = slice(start, start + COLUMNS)
        output = scale * jnp.dot(
            hidden, down_ref[0, :, part], preferred_element_type=jnp.float32
        )
        shape = (groups, tok_rows, COLUMNS)
        own_out[:, side, :, part] = output[:rows].reshape(shape)
        own_out[:, 1 - side, :, part] = output[rows : 2 * rows].reshape(shape)
        other = output[2 * rows :].astype(jnp.bfloat16)
        other_out[:, side, :, part] = other[:rows].reshape(shape)
        other_out[:, 1 - side, :, part] = other[rows:].reshape(shape)


def per_device(tokens, routes, route_weights, gate_weight, up_weight, down_weight):
    tok_rows, width = tokens.shape
    nodes = lax.axis_size("node")
    devs = lax.axis_size("dev")
    groups = devs // 2
    experts = nodes * (devs // SPLIT)
    wide = width + -(-experts // LANES) * LANES
    vmem = pl.BlockSpec(memory_space=pltpu.VMEM)
    swap = [(i, i ^ 1) for i in range(nodes)]
    beside = [(i, i ^ 1) for i in range(devs)]
    lines = [list(range(side, devs, 2)) for side in range(2)]

    packed = pl.pallas_call(
        pack_kernel,
        out_shape=pltpu.VMEM((groups, tok_rows, wide), jnp.bfloat16),
        in_specs=[vmem] * 3,
        out_specs=vmem,
        name="pack",
    )(tokens, routes.T, route_weights)
    near = lax.all_to_all(
        packed, "dev", split_axis=0, concat_axis=0, tiled=True, axis_index_groups=lines
    )
    near, gate_source, up_source = lax.optimization_barrier((near, gate_weight, up_weight))
    far = lax.ppermute(near, "dev", beside)
    near_other = lax.ppermute(near, "node", swap)
    piece = 2 * groups * tok_rows * wide
    weight_bytes = 2 * gate_weight.size
    gate_held = load(gate_source, 3 * piece + weight_bytes)
    up_held = load(up_source, 3 * piece + 2 * weight_bytes)
    far, near_other, gate_held, up_held, down_source = lax.optimization_barrier(
        (far, near_other, gate_held, up_held, down_weight)
    )
    far_other = lax.ppermute(far, "node", swap)
    down_held = load(down_source, 4 * piece + 3 * weight_bytes)
    shape = (groups, 2, tok_rows, width)
    own_out, other_out = pl.pallas_call(
        expert_kernel,
        out_shape=(
            jax.ShapeDtypeStruct(shape, jnp.float32),
            jax.ShapeDtypeStruct(shape, jnp.bfloat16),
        ),
        in_specs=[vmem] * 7,
        out_specs=(vmem, vmem),
        compiler_params=pltpu.CompilerParams(vmem_limit_bytes=EXPERT_LIMIT),
        name="expert",
    )(near, far, near_other, far_other, gate_held, up_held, down_held)
    arrived = lax.ppermute(other_out, "node", swap)
    partial = (own_out + arrived.astype(jnp.float32)).astype(jnp.bfloat16)
    returned = lax.all_to_all(
        partial.reshape(devs, tok_rows, width), "dev", split_axis=0, concat_axis=0, tiled=True
    )
    return jnp.sum(returned.astype(jnp.float32), axis=0).astype(jnp.bfloat16)


def solution(mesh):
    rows = P(("replica", "node", "dev"), None)
    shards = P(("node", "dev"), None, None)
    return jax.shard_map(
        per_device,
        mesh=mesh,
        in_specs=(rows, rows, rows, shards, shards, shards),
        out_specs=rows,
        check_vma=False,
    )
```

```python
import jax
import jax.numpy as jnp
from jax import lax
from jax.experimental import pallas as pl
from jax.experimental.pallas import tpu as pltpu
from jax.sharding import PartitionSpec as P

SPLIT = 8
LANES = 128
VMEM_LIMIT = 32 * 1024 * 1024
SPARE = 2048
SPACER_LIMIT = 38 * 1024 * 1024
COLUMNS = 1024


def pack_kernel(tokens_ref, routes_ref, weights_ref, packed_ref, spare_ref):
    rows, width = tokens_ref.shape
    copies = packed_ref.shape[0]
    extra = packed_ref.shape[2] - width
    columns = lax.broadcasted_iota(jnp.int32, (rows, extra), 1)
    combine = jnp.zeros((rows, extra), jnp.float32)
    for k in range(routes_ref.shape[0]):
        route = jnp.concatenate([routes_ref[k : k + 1, r : r + 1] for r in range(rows)], axis=0)
        weight = weights_ref[:, k : k + 1].astype(jnp.float32)
        combine += jnp.where(columns == route, weight, 0.0)
    combine = combine.astype(jnp.bfloat16)
    for c in range(copies):
        packed_ref[c, :, :width] = tokens_ref[...]
        packed_ref[c, :, width:] = combine


def spacer_kernel(packed_ref, spare_hbm, mark_ref):
    mark_ref[...] = jnp.zeros_like(mark_ref)


def expert_kernel(own_ref, other_ref, gate_ref, up_ref, down_ref, mark_ref, own_out, other_out):
    devs, tok_rows, wide = own_ref.shape
    _, width, hidden_units = gate_ref.shape
    rows = devs * tok_rows

    def tokens_part(part):
        halves = [ref[:, :, part] for ref in (own_ref, other_ref)]
        return jnp.concatenate([half.reshape(rows, half.shape[2]) for half in halves], axis=0)

    expert = lax.axis_index("node") * (lax.axis_size("dev") // SPLIT) + lax.axis_index("dev") // SPLIT
    combine = tokens_part(slice(width, wide)).astype(jnp.float32)
    columns = lax.broadcasted_iota(jnp.int32, combine.shape, 1)
    scale = jnp.sum(jnp.where(columns == expert, combine, 0.0), axis=1, keepdims=True)
    gate = jnp.zeros((2 * rows, hidden_units), jnp.float32)
    upper = jnp.zeros((2 * rows, hidden_units), jnp.float32)
    for start in range(0, width, COLUMNS):
        part = slice(start, start + COLUMNS)
        block = tokens_part(part)
        gate += jnp.dot(block, gate_ref[0, part, :], preferred_element_type=jnp.float32)
        upper += jnp.dot(block, up_ref[0, part, :], preferred_element_type=jnp.float32)
    hidden = (gate / (1.0 + jnp.exp(-gate)) * upper).astype(jnp.bfloat16)
    for start in range(0, width, COLUMNS):
        part = slice(start, start + COLUMNS)
        output = scale * jnp.dot(
            hidden, down_ref[0, :, part], preferred_element_type=jnp.float32
        )
        own_out[:, :, part] = output[:rows].reshape(devs, tok_rows, COLUMNS)
        other = output[rows:].astype(jnp.bfloat16)
        other_out[:, :, part] = other.reshape(devs, tok_rows, COLUMNS)


def per_device(tokens, routes, route_weights, gate_weight, up_weight, down_weight):
    tok_rows, width = tokens.shape
    nodes = lax.axis_size("node")
    devs = lax.axis_size("dev")
    per_node = devs // SPLIT
    experts = nodes * per_node
    wide = width + -(-experts // LANES) * LANES
    vmem = pl.BlockSpec(memory_space=pltpu.VMEM)
    swap = [(i, i ^ 1) for i in range(nodes)]

    packed, spare = pl.pallas_call(
        pack_kernel,
        out_shape=(
            pltpu.VMEM((devs, tok_rows, wide), jnp.bfloat16),
            jax.ShapeDtypeStruct((SPARE, width), jnp.bfloat16),
        ),
        in_specs=[vmem] * 3,
        out_specs=(vmem, pl.BlockSpec(memory_space=pltpu.HBM)),
        name="pack",
    )(tokens, routes.T, route_weights)
    mark = pl.pallas_call(
        spacer_kernel,
        out_shape=pltpu.VMEM((8, LANES), jnp.float32),
        in_specs=[vmem, pl.BlockSpec(memory_space=pltpu.HBM)],
        out_specs=vmem,
        compiler_params=pltpu.CompilerParams(vmem_limit_bytes=SPACER_LIMIT),
        name="spacer",
    )(packed, spare)
    packed, mark = lax.optimization_barrier((packed, mark))
    own = lax.all_to_all(packed, "dev", split_axis=0, concat_axis=0, tiled=True)
    other = lax.ppermute(own, "node", swap)
    own_out, other_out = pl.pallas_call(
        expert_kernel,
        out_shape=(
            jax.ShapeDtypeStruct((devs, tok_rows, width), jnp.float32),
            jax.ShapeDtypeStruct((devs, tok_rows, width), jnp.bfloat16),
        ),
        in_specs=[vmem] * 6,
        out_specs=(vmem, vmem),
        compiler_params=pltpu.CompilerParams(vmem_limit_bytes=VMEM_LIMIT),
        name="expert",
    )(own, other, gate_weight, up_weight, down_weight, mark)
    arrived = lax.ppermute(other_out, "node", swap)
    partial = (own_out + arrived.astype(jnp.float32)).astype(jnp.bfloat16)
    returned = lax.all_to_all(partial, "dev", split_axis=0, concat_axis=0, tiled=True)
    return jnp.sum(returned.astype(jnp.float32), axis=0).astype(jnp.bfloat16)


def solution(mesh):
    rows = P(("replica", "node", "dev"), None)
    shards = P(("node", "dev"), None, None)
    return jax.shard_map(
        per_device,
        mesh=mesh,
        in_specs=(rows, rows, rows, shards, shards, shards),
        out_specs=rows,
        check_vma=False,
    )
```

```python
import jax
import jax.numpy as jnp
from jax import lax
from jax.experimental import pallas as pl
from jax.experimental.pallas import tpu as pltpu
from jax.sharding import PartitionSpec as P

SPLIT = 8
LANES = 128
VMEM_LIMIT = 32 * 1024 * 1024
SPARE = 2048
SPACER_LIMIT = 38 * 1024 * 1024
COLUMNS = 1024
RING_OF_8 = (5, 4, 3, 2, 7, 6, 1, 0)


def pack_kernel(tokens_ref, routes_ref, weights_ref, packed_ref, spare_ref):
    rows, width = tokens_ref.shape
    copies = packed_ref.shape[0]
    extra = packed_ref.shape[2] - width
    columns = lax.broadcasted_iota(jnp.int32, (rows, extra), 1)
    combine = jnp.zeros((rows, extra), jnp.float32)
    for k in range(routes_ref.shape[0]):
        route = jnp.concatenate([routes_ref[k : k + 1, r : r + 1] for r in range(rows)], axis=0)
        weight = weights_ref[:, k : k + 1].astype(jnp.float32)
        combine += jnp.where(columns == route, weight, 0.0)
    combine = combine.astype(jnp.bfloat16)
    for c in range(copies):
        packed_ref[c, :, :width] = tokens_ref[...]
        packed_ref[c, :, width:] = combine


def spacer_kernel(packed_ref, spare_hbm, mark_ref):
    mark_ref[...] = jnp.zeros_like(mark_ref)


def expert_kernel(own_ref, other_ref, gate_ref, up_ref, down_ref, mark_ref, own_out, other_out):
    devs, tok_rows, wide = own_ref.shape
    _, width, hidden_units = gate_ref.shape
    rows = devs * tok_rows

    def tokens_part(part):
        halves = [ref[:, :, part] for ref in (own_ref, other_ref)]
        return jnp.concatenate([half.reshape(rows, half.shape[2]) for half in halves], axis=0)

    expert = lax.axis_index("node") * (lax.axis_size("dev") // SPLIT) + lax.axis_index("dev") // SPLIT
    combine = tokens_part(slice(width, wide)).astype(jnp.float32)
    columns = lax.broadcasted_iota(jnp.int32, combine.shape, 1)
    scale = jnp.sum(jnp.where(columns == expert, combine, 0.0), axis=1, keepdims=True)
    gate = jnp.zeros((2 * rows, hidden_units), jnp.float32)
    upper = jnp.zeros((2 * rows, hidden_units), jnp.float32)
    for start in range(0, width, COLUMNS):
        part = slice(start, start + COLUMNS)
        block = tokens_part(part)
        gate += jnp.dot(block, gate_ref[0, part, :], preferred_element_type=jnp.float32)
        upper += jnp.dot(block, up_ref[0, part, :], preferred_element_type=jnp.float32)
    hidden = (gate / (1.0 + jnp.exp(-gate)) * upper).astype(jnp.bfloat16)
    for start in range(0, width, COLUMNS):
        part = slice(start, start + COLUMNS)
        output = scale * jnp.dot(
            hidden, down_ref[0, :, part], preferred_element_type=jnp.float32
        )
        own_out[:, :, part] = output[:rows].reshape(devs, tok_rows, COLUMNS)
        other = output[rows:].astype(jnp.bfloat16)
        other_out[:, :, part] = other.reshape(devs, tok_rows, COLUMNS)


def per_device(tokens, routes, route_weights, gate_weight, up_weight, down_weight):
    tok_rows, width = tokens.shape
    nodes = lax.axis_size("node")
    devs = lax.axis_size("dev")
    per_node = devs // SPLIT
    experts = nodes * per_node
    wide = width + -(-experts // LANES) * LANES
    vmem = pl.BlockSpec(memory_space=pltpu.VMEM)
    swap = [(i, i ^ 1) for i in range(nodes)]
    order = [list(RING_OF_8 if devs == len(RING_OF_8) else range(devs))]

    packed, spare = pl.pallas_call(
        pack_kernel,
        out_shape=(
            pltpu.VMEM((devs, tok_rows, wide), jnp.bfloat16),
            jax.ShapeDtypeStruct((SPARE, width), jnp.bfloat16),
        ),
        in_specs=[vmem] * 3,
        out_specs=(vmem, pl.BlockSpec(memory_space=pltpu.HBM)),
        name="pack",
    )(tokens, routes.T, route_weights)
    mark = pl.pallas_call(
        spacer_kernel,
        out_shape=pltpu.VMEM((8, LANES), jnp.float32),
        in_specs=[vmem, pl.BlockSpec(memory_space=pltpu.HBM)],
        out_specs=vmem,
        compiler_params=pltpu.CompilerParams(vmem_limit_bytes=SPACER_LIMIT),
        name="spacer",
    )(packed, spare)
    packed, mark = lax.optimization_barrier((packed, mark))
    own = lax.all_to_all(
        packed, "dev", split_axis=0, concat_axis=0, tiled=True, axis_index_groups=order
    )
    other = lax.ppermute(own, "node", swap)
    own_out, other_out = pl.pallas_call(
        expert_kernel,
        out_shape=(
            jax.ShapeDtypeStruct((devs, tok_rows, width), jnp.float32),
            jax.ShapeDtypeStruct((devs, tok_rows, width), jnp.bfloat16),
        ),
        in_specs=[vmem] * 6,
        out_specs=(vmem, vmem),
        compiler_params=pltpu.CompilerParams(vmem_limit_bytes=VMEM_LIMIT),
        name="expert",
    )(own, other, gate_weight, up_weight, down_weight, mark)
    arrived = lax.ppermute(other_out, "node", swap)
    partial = (own_out + arrived.astype(jnp.float32)).astype(jnp.bfloat16)
    returned = lax.all_to_all(
        partial, "dev", split_axis=0, concat_axis=0, tiled=True, axis_index_groups=order
    )
    return jnp.sum(returned.astype(jnp.float32), axis=0).astype(jnp.bfloat16)


def solution(mesh):
    rows = P(("replica", "node", "dev"), None)
    shards = P(("node", "dev"), None, None)
    return jax.shard_map(
        per_device,
        mesh=mesh,
        in_specs=(rows, rows, rows, shards, shards, shards),
        out_specs=rows,
        check_vma=False,
    )
```

```python
import jax
import jax.numpy as jnp
from jax import lax
from jax.experimental import pallas as pl
from jax.experimental.pallas import tpu as pltpu
from jax.sharding import PartitionSpec as P

SPLIT = 8
LANES = 128
VMEM_LIMIT = 32 * 1024 * 1024
SPARE = 2048
SPACER_LIMIT = 38 * 1024 * 1024
COLUMNS = 1024
SEND_ORDERS = ((5, 3, 4, 0, 7, 1, 2, 6), (5, 7, 4, 0, 1, 3, 2, 6))
RETURN_ORDERS = ((5, 4, 3, 2, 7, 6, 1, 0), (4, 0, 2, 7, 1, 6, 5, 3))


def pack_kernel(tokens_ref, routes_ref, weights_ref, packed_ref, spare_ref):
    rows, width = tokens_ref.shape
    copies = packed_ref.shape[0]
    extra = packed_ref.shape[2] - width
    columns = lax.broadcasted_iota(jnp.int32, (rows, extra), 1)
    combine = jnp.zeros((rows, extra), jnp.float32)
    for k in range(routes_ref.shape[0]):
        route = jnp.concatenate([routes_ref[k : k + 1, r : r + 1] for r in range(rows)], axis=0)
        weight = weights_ref[:, k : k + 1].astype(jnp.float32)
        combine += jnp.where(columns == route, weight, 0.0)
    combine = combine.astype(jnp.bfloat16)
    for c in range(copies):
        packed_ref[c, :, :width] = tokens_ref[...]
        packed_ref[c, :, width:] = combine


def spacer_kernel(packed_ref, spare_hbm, mark_ref):
    mark_ref[...] = jnp.zeros_like(mark_ref)


def reorder_matrix(devs, tok_rows):
    half = devs * tok_rows
    shape = (2 * half, 2 * half)
    place = lax.broadcasted_iota(jnp.int32, shape, 0)
    source = lax.broadcasted_iota(jnp.int32, shape, 1)
    node = lax.axis_index("node")
    core = jnp.where(place < half, node, 1 - node)
    wanted = jnp.zeros(shape, jnp.int32)
    for c in range(2):
        for q in range(devs):
            held = SEND_ORDERS[c].index(RETURN_ORDERS[c][q])
            here = (core == c) & (place % half // tok_rows == q)
            wanted = jnp.where(here, held * tok_rows, wanted)
    wanted += place // half * half + place % tok_rows
    return (source == wanted).astype(jnp.bfloat16)


def expert_kernel(own_ref, other_ref, gate_ref, up_ref, down_ref, mark_ref, own_out, other_out):
    devs, tok_rows, wide = own_ref.shape
    _, width, hidden_units = gate_ref.shape
    rows = devs * tok_rows

    def tokens_part(part):
        halves = [ref[:, :, part] for ref in (own_ref, other_ref)]
        return jnp.concatenate([half.reshape(rows, half.shape[2]) for half in halves], axis=0)

    expert = lax.axis_index("node") * (lax.axis_size("dev") // SPLIT) + lax.axis_index("dev") // SPLIT
    combine = tokens_part(slice(width, wide))
    if devs == len(SEND_ORDERS[0]):
        reorder = reorder_matrix(devs, tok_rows)
        combine = jnp.dot(reorder, combine, preferred_element_type=jnp.float32)
    combine = combine.astype(jnp.float32)
    columns = lax.broadcasted_iota(jnp.int32, combine.shape, 1)
    scale = jnp.sum(jnp.where(columns == expert, combine, 0.0), axis=1, keepdims=True)
    gate = jnp.zeros((2 * rows, hidden_units), jnp.float32)
    upper = jnp.zeros((2 * rows, hidden_units), jnp.float32)
    for start in range(0, width, COLUMNS):
        part = slice(start, start + COLUMNS)
        block = tokens_part(part)
        gate += jnp.dot(block, gate_ref[0, part, :], preferred_element_type=jnp.float32)
        upper += jnp.dot(block, up_ref[0, part, :], preferred_element_type=jnp.float32)
    hidden = (gate / (1.0 + jnp.exp(-gate)) * upper).astype(jnp.bfloat16)
    if devs == len(SEND_ORDERS[0]):
        hidden = jnp.dot(reorder, hidden, preferred_element_type=jnp.float32).astype(jnp.bfloat16)
    for start in range(0, width, COLUMNS):
        part = slice(start, start + COLUMNS)
        output = scale * jnp.dot(
            hidden, down_ref[0, :, part], preferred_element_type=jnp.float32
        )
        own_out[:, :, part] = output[:rows].reshape(devs, tok_rows, COLUMNS)
        other = output[rows:].astype(jnp.bfloat16)
        other_out[:, :, part] = other.reshape(devs, tok_rows, COLUMNS)


def per_device(tokens, routes, route_weights, gate_weight, up_weight, down_weight):
    tok_rows, width = tokens.shape
    nodes = lax.axis_size("node")
    devs = lax.axis_size("dev")
    per_node = devs // SPLIT
    experts = nodes * per_node
    wide = width + -(-experts // LANES) * LANES
    vmem = pl.BlockSpec(memory_space=pltpu.VMEM)
    swap = [(i, i ^ 1) for i in range(nodes)]
    if devs == len(SEND_ORDERS[0]):
        orders = (SEND_ORDERS, RETURN_ORDERS)
    else:
        orders = ((tuple(range(devs)),) * nodes,) * 2
    send_groups, return_groups = (
        [[node * devs + dev for dev in order[node]] for node in range(nodes)] for order in orders
    )

    packed, spare = pl.pallas_call(
        pack_kernel,
        out_shape=(
            pltpu.VMEM((devs, tok_rows, wide), jnp.bfloat16),
            jax.ShapeDtypeStruct((SPARE, width), jnp.bfloat16),
        ),
        in_specs=[vmem] * 3,
        out_specs=(vmem, pl.BlockSpec(memory_space=pltpu.HBM)),
        name="pack",
    )(tokens, routes.T, route_weights)
    mark = pl.pallas_call(
        spacer_kernel,
        out_shape=pltpu.VMEM((8, LANES), jnp.float32),
        in_specs=[vmem, pl.BlockSpec(memory_space=pltpu.HBM)],
        out_specs=vmem,
        compiler_params=pltpu.CompilerParams(vmem_limit_bytes=SPACER_LIMIT),
        name="spacer",
    )(packed, spare)
    packed, mark = lax.optimization_barrier((packed, mark))
    own = lax.all_to_all(
        packed, ("node", "dev"), split_axis=0, concat_axis=0, tiled=True,
        axis_index_groups=send_groups,
    )
    other = lax.ppermute(own, "node", swap)
    own_out, other_out = pl.pallas_call(
        expert_kernel,
        out_shape=(
            jax.ShapeDtypeStruct((devs, tok_rows, width), jnp.float32),
            jax.ShapeDtypeStruct((devs, tok_rows, width), jnp.bfloat16),
        ),
        in_specs=[vmem] * 6,
        out_specs=(vmem, vmem),
        compiler_params=pltpu.CompilerParams(vmem_limit_bytes=VMEM_LIMIT),
        name="expert",
    )(own, other, gate_weight, up_weight, down_weight, mark)
    arrived = lax.ppermute(other_out, "node", swap)
    partial = (own_out + arrived.astype(jnp.float32)).astype(jnp.bfloat16)
    returned = lax.all_to_all(
        partial, ("node", "dev"), split_axis=0, concat_axis=0, tiled=True,
        axis_index_groups=return_groups,
    )
    return jnp.sum(returned.astype(jnp.float32), axis=0).astype(jnp.bfloat16)


def solution(mesh):
    rows = P(("replica", "node", "dev"), None)
    shards = P(("node", "dev"), None, None)
    return jax.shard_map(
        per_device,
        mesh=mesh,
        in_specs=(rows, rows, rows, shards, shards, shards),
        out_specs=rows,
        check_vma=False,
    )
```

```python
import jax
import jax.numpy as jnp
from jax import lax
from jax.experimental import pallas as pl
from jax.experimental.pallas import tpu as pltpu
from jax.sharding import PartitionSpec as P

SPLIT = 8
LANES = 128
VMEM_LIMIT = 32 * 1024 * 1024
SPARE = 2048
SPACER_LIMIT = 38 * 1024 * 1024
COLUMNS = 1024
SEND_ORDERS = ((5, 7, 4, 0, 3, 1, 2, 6), (5, 0, 3, 2, 4, 1, 7, 6))
RETURN_ORDERS = ((5, 4, 3, 0, 7, 6, 1, 2), (4, 0, 2, 7, 1, 6, 5, 3))


def pack_kernel(tokens_ref, routes_ref, weights_ref, packed_ref, spare_ref):
    rows, width = tokens_ref.shape
    copies = packed_ref.shape[0]
    extra = packed_ref.shape[2] - width
    columns = lax.broadcasted_iota(jnp.int32, (rows, extra), 1)
    combine = jnp.zeros((rows, extra), jnp.float32)
    for k in range(routes_ref.shape[0]):
        route = jnp.concatenate([routes_ref[k : k + 1, r : r + 1] for r in range(rows)], axis=0)
        weight = weights_ref[:, k : k + 1].astype(jnp.float32)
        combine += jnp.where(columns == route, weight, 0.0)
    combine = combine.astype(jnp.bfloat16)
    for c in range(copies):
        packed_ref[c, :, :width] = tokens_ref[...]
        packed_ref[c, :, width:] = combine


def spacer_kernel(packed_ref, spare_hbm, mark_ref):
    mark_ref[...] = jnp.zeros_like(mark_ref)


def reorder_matrix(devs, tok_rows):
    half = devs * tok_rows
    shape = (2 * half, 2 * half)
    place = lax.broadcasted_iota(jnp.int32, shape, 0)
    source = lax.broadcasted_iota(jnp.int32, shape, 1)
    node = lax.axis_index("node")
    core = jnp.where(place < half, node, 1 - node)
    wanted = jnp.zeros(shape, jnp.int32)
    for c in range(2):
        for q in range(devs):
            held = SEND_ORDERS[c].index(RETURN_ORDERS[c][q])
            here = (core == c) & (place % half // tok_rows == q)
            wanted = jnp.where(here, held * tok_rows, wanted)
    wanted += place // half * half + place % tok_rows
    return (source == wanted).astype(jnp.bfloat16)


def expert_kernel(own_ref, other_ref, gate_ref, up_ref, down_ref, mark_ref, own_out, other_out):
    devs, tok_rows, wide = own_ref.shape
    _, width, hidden_units = gate_ref.shape
    rows = devs * tok_rows

    def tokens_part(part):
        halves = [ref[:, :, part] for ref in (own_ref, other_ref)]
        return jnp.concatenate([half.reshape(rows, half.shape[2]) for half in halves], axis=0)

    expert = lax.axis_index("node") * (lax.axis_size("dev") // SPLIT) + lax.axis_index("dev") // SPLIT
    combine = tokens_part(slice(width, wide))
    if devs == len(SEND_ORDERS[0]):
        reorder = reorder_matrix(devs, tok_rows)
        combine = jnp.dot(reorder, combine, preferred_element_type=jnp.float32)
    combine = combine.astype(jnp.float32)
    columns = lax.broadcasted_iota(jnp.int32, combine.shape, 1)
    scale = jnp.sum(jnp.where(columns == expert, combine, 0.0), axis=1, keepdims=True)
    gate = jnp.zeros((2 * rows, hidden_units), jnp.float32)
    upper = jnp.zeros((2 * rows, hidden_units), jnp.float32)
    for start in range(0, width, COLUMNS):
        part = slice(start, start + COLUMNS)
        block = tokens_part(part)
        gate += jnp.dot(block, gate_ref[0, part, :], preferred_element_type=jnp.float32)
        upper += jnp.dot(block, up_ref[0, part, :], preferred_element_type=jnp.float32)
    hidden = (gate / (1.0 + jnp.exp(-gate)) * upper).astype(jnp.bfloat16)
    if devs == len(SEND_ORDERS[0]):
        hidden = jnp.dot(reorder, hidden, preferred_element_type=jnp.float32).astype(jnp.bfloat16)
    for start in range(0, width, COLUMNS):
        part = slice(start, start + COLUMNS)
        output = scale * jnp.dot(
            hidden, down_ref[0, :, part], preferred_element_type=jnp.float32
        )
        own_out[:, :, part] = output[:rows].reshape(devs, tok_rows, COLUMNS)
        other = output[rows:].astype(jnp.bfloat16)
        other_out[:, :, part] = other.reshape(devs, tok_rows, COLUMNS)


def per_device(tokens, routes, route_weights, gate_weight, up_weight, down_weight):
    tok_rows, width = tokens.shape
    nodes = lax.axis_size("node")
    devs = lax.axis_size("dev")
    per_node = devs // SPLIT
    experts = nodes * per_node
    wide = width + -(-experts // LANES) * LANES
    vmem = pl.BlockSpec(memory_space=pltpu.VMEM)
    swap = [(i, i ^ 1) for i in range(nodes)]
    if devs == len(SEND_ORDERS[0]):
        orders = (SEND_ORDERS, RETURN_ORDERS)
    else:
        orders = ((tuple(range(devs)),) * nodes,) * 2
    send_groups, return_groups = (
        [[node * devs + dev for dev in order[node]] for node in range(nodes)] for order in orders
    )

    packed, spare = pl.pallas_call(
        pack_kernel,
        out_shape=(
            pltpu.VMEM((devs, tok_rows, wide), jnp.bfloat16),
            jax.ShapeDtypeStruct((SPARE, width), jnp.bfloat16),
        ),
        in_specs=[vmem] * 3,
        out_specs=(vmem, pl.BlockSpec(memory_space=pltpu.HBM)),
        name="pack",
    )(tokens, routes.T, route_weights)
    mark = pl.pallas_call(
        spacer_kernel,
        out_shape=pltpu.VMEM((8, LANES), jnp.float32),
        in_specs=[vmem, pl.BlockSpec(memory_space=pltpu.HBM)],
        out_specs=vmem,
        compiler_params=pltpu.CompilerParams(vmem_limit_bytes=SPACER_LIMIT),
        name="spacer",
    )(packed, spare)
    packed, mark = lax.optimization_barrier((packed, mark))
    own = lax.all_to_all(
        packed, ("node", "dev"), split_axis=0, concat_axis=0, tiled=True,
        axis_index_groups=send_groups,
    )
    other = lax.ppermute(own, "node", swap)
    own_out, other_out = pl.pallas_call(
        expert_kernel,
        out_shape=(
            jax.ShapeDtypeStruct((devs, tok_rows, width), jnp.float32),
            jax.ShapeDtypeStruct((devs, tok_rows, width), jnp.bfloat16),
        ),
        in_specs=[vmem] * 6,
        out_specs=(vmem, vmem),
        compiler_params=pltpu.CompilerParams(vmem_limit_bytes=VMEM_LIMIT),
        name="expert",
    )(own, other, gate_weight, up_weight, down_weight, mark)
    arrived = lax.ppermute(other_out, "node", swap)
    partial = (own_out + arrived.astype(jnp.float32)).astype(jnp.bfloat16)
    returned = lax.all_to_all(
        partial, ("node", "dev"), split_axis=0, concat_axis=0, tiled=True,
        axis_index_groups=return_groups,
    )
    return jnp.sum(returned.astype(jnp.float32), axis=0).astype(jnp.bfloat16)


def solution(mesh):
    rows = P(("replica", "node", "dev"), None)
    shards = P(("node", "dev"), None, None)
    return jax.shard_map(
        per_device,
        mesh=mesh,
        in_specs=(rows, rows, rows, shards, shards, shards),
        out_specs=rows,
        check_vma=False,
    )
```

```python
import jax
import jax.numpy as jnp
from jax import lax
from jax.experimental import pallas as pl
from jax.experimental.pallas import tpu as pltpu
from jax.sharding import PartitionSpec as P

SPLIT = 8
LANES = 128
VMEM_LIMIT = 32 * 1024 * 1024
SPARE = 2048
SPACER_LIMIT = 38 * 1024 * 1024
COLUMNS = 1024
SEND_ORDERS = ((5, 7, 4, 0, 3, 1, 2, 6), (5, 0, 3, 2, 4, 1, 7, 6))
RETURN_ORDERS = ((5, 4, 3, 0, 7, 6, 1, 2), (4, 0, 2, 7, 1, 6, 5, 3))


def pack_kernel(tokens_ref, routes_ref, weights_ref, packed_ref, spare_ref):
    rows, width = tokens_ref.shape
    copies = packed_ref.shape[0]
    extra = packed_ref.shape[2] - width
    columns = lax.broadcasted_iota(jnp.int32, (rows, extra), 1)
    combine = jnp.zeros((rows, extra), jnp.float32)
    for k in range(routes_ref.shape[0]):
        route = jnp.concatenate([routes_ref[k : k + 1, r : r + 1] for r in range(rows)], axis=0)
        weight = weights_ref[:, k : k + 1].astype(jnp.float32)
        combine += jnp.where(columns == route, weight, 0.0)
    combine = combine.astype(jnp.bfloat16)
    for c in range(copies):
        packed_ref[c, :, :width] = tokens_ref[...]
        packed_ref[c, :, width:] = combine


def spacer_kernel(packed_ref, spare_hbm, mark_ref):
    mark_ref[...] = jnp.zeros_like(mark_ref)


def reorder_matrix(devs, tok_rows):
    half = devs * tok_rows
    shape = (2 * half, 2 * half)
    place = lax.broadcasted_iota(jnp.int32, shape, 0)
    source = lax.broadcasted_iota(jnp.int32, shape, 1)
    node = lax.axis_index("node")
    core = jnp.where(place < half, node, 1 - node)
    wanted = jnp.zeros(shape, jnp.int32)
    for c in range(2):
        for q in range(devs):
            held = SEND_ORDERS[c].index(RETURN_ORDERS[c][q])
            here = (core == c) & (place % half // tok_rows == q)
            wanted = jnp.where(here, held * tok_rows, wanted)
    wanted += place // half * half + place % tok_rows
    return (source == wanted).astype(jnp.bfloat16)


def expert_kernel(own_ref, other_ref, gate_ref, up_ref, down_ref, mark_ref, own_out, other_out):
    devs, tok_rows, wide = own_ref.shape
    _, width, hidden_units = gate_ref.shape
    rows = devs * tok_rows

    def tokens_part(part):
        halves = [ref[:, :, part] for ref in (own_ref, other_ref)]
        return jnp.concatenate([half.reshape(rows, half.shape[2]) for half in halves], axis=0)

    expert = lax.axis_index("node") * (lax.axis_size("dev") // SPLIT) + lax.axis_index("dev") // SPLIT
    combine = tokens_part(slice(width, wide))
    if devs == len(SEND_ORDERS[0]):
        reorder = reorder_matrix(devs, tok_rows)
        combine = jnp.dot(reorder, combine, preferred_element_type=jnp.float32)
    combine = combine.astype(jnp.float32)
    columns = lax.broadcasted_iota(jnp.int32, combine.shape, 1)
    scale = jnp.sum(jnp.where(columns == expert, combine, 0.0), axis=1, keepdims=True)
    gate = jnp.zeros((2 * rows, hidden_units), jnp.float32)
    upper = jnp.zeros((2 * rows, hidden_units), jnp.float32)
    for start in range(0, width, COLUMNS):
        part = slice(start, start + COLUMNS)
        block = tokens_part(part)
        gate += jnp.dot(block, gate_ref[0, part, :], preferred_element_type=jnp.float32)
        upper += jnp.dot(block, up_ref[0, part, :], preferred_element_type=jnp.float32)
    hidden = (gate / (1.0 + jnp.exp(-gate)) * upper).astype(jnp.bfloat16)
    if devs == len(SEND_ORDERS[0]):
        hidden = jnp.dot(reorder, hidden, preferred_element_type=jnp.float32).astype(jnp.bfloat16)
    for start in range(0, width, COLUMNS):
        part = slice(start, start + COLUMNS)
        output = scale * jnp.dot(
            hidden, down_ref[0, :, part], preferred_element_type=jnp.float32
        )
        own_out[:, part] = output[:rows]
        other_out[:, part] = output[rows:].astype(jnp.bfloat16)


def per_device(tokens, routes, route_weights, gate_weight, up_weight, down_weight):
    tok_rows, width = tokens.shape
    nodes = lax.axis_size("node")
    devs = lax.axis_size("dev")
    per_node = devs // SPLIT
    experts = nodes * per_node
    wide = width + -(-experts // LANES) * LANES
    vmem = pl.BlockSpec(memory_space=pltpu.VMEM)
    swap = [(i, i ^ 1) for i in range(nodes)]
    if devs == len(SEND_ORDERS[0]):
        orders = (SEND_ORDERS, RETURN_ORDERS)
    else:
        orders = ((tuple(range(devs)),) * nodes,) * 2
    send_groups, return_groups = (
        [[node * devs + dev for dev in order[node]] for node in range(nodes)] for order in orders
    )

    packed, spare = pl.pallas_call(
        pack_kernel,
        out_shape=(
            pltpu.VMEM((devs, tok_rows, wide), jnp.bfloat16),
            jax.ShapeDtypeStruct((SPARE, width), jnp.bfloat16),
        ),
        in_specs=[vmem] * 3,
        out_specs=(vmem, pl.BlockSpec(memory_space=pltpu.HBM)),
        name="pack",
    )(tokens, routes.T, route_weights)
    mark = pl.pallas_call(
        spacer_kernel,
        out_shape=pltpu.VMEM((8, LANES), jnp.float32),
        in_specs=[vmem, pl.BlockSpec(memory_space=pltpu.HBM)],
        out_specs=vmem,
        compiler_params=pltpu.CompilerParams(vmem_limit_bytes=SPACER_LIMIT),
        name="spacer",
    )(packed, spare)
    packed, mark = lax.optimization_barrier((packed, mark))
    own = lax.all_to_all(
        packed, ("node", "dev"), split_axis=0, concat_axis=0, tiled=True,
        axis_index_groups=send_groups,
    )
    other = lax.ppermute(own, "node", swap)
    own_out, other_out = pl.pallas_call(
        expert_kernel,
        out_shape=(
            jax.ShapeDtypeStruct((devs * tok_rows, width), jnp.float32),
            jax.ShapeDtypeStruct((devs * tok_rows, width), jnp.bfloat16),
        ),
        in_specs=[vmem] * 6,
        out_specs=(vmem, vmem),
        compiler_params=pltpu.CompilerParams(vmem_limit_bytes=VMEM_LIMIT),
        name="expert",
    )(own, other, gate_weight, up_weight, down_weight, mark)
    arrived = lax.ppermute(other_out, "node", swap)
    partial = (own_out + arrived.astype(jnp.float32)).astype(jnp.bfloat16)
    partial = partial.reshape(devs, tok_rows, width)
    returned = lax.all_to_all(
        partial, ("node", "dev"), split_axis=0, concat_axis=0, tiled=True,
        axis_index_groups=return_groups,
    )
    return jnp.sum(returned.astype(jnp.float32), axis=0).astype(jnp.bfloat16)


def solution(mesh):
    rows = P(("replica", "node", "dev"), None)
    shards = P(("node", "dev"), None, None)
    return jax.shard_map(
        per_device,
        mesh=mesh,
        in_specs=(rows, rows, rows, shards, shards, shards),
        out_specs=rows,
        check_vma=False,
    )
```

```python
import jax
import jax.numpy as jnp
from jax import lax
from jax.experimental import pallas as pl
from jax.experimental.pallas import tpu as pltpu
from jax.sharding import PartitionSpec as P

SPLIT = 8
LANES = 128
VMEM_LIMIT = 32 * 1024 * 1024
SPARE = 2048
SPACER_LIMIT = 38 * 1024 * 1024
COLUMNS = 1024
SEND_ORDERS = ((5, 7, 4, 0, 3, 1, 2, 6), (5, 6, 0, 2, 4, 3, 7, 1))
RETURN_ORDERS = ((5, 4, 3, 0, 7, 6, 1, 2), (4, 0, 2, 7, 1, 6, 5, 3))


def pack_kernel(tokens_ref, routes_ref, weights_ref, packed_ref, spare_ref):
    rows, width = tokens_ref.shape
    copies = packed_ref.shape[0]
    extra = packed_ref.shape[2] - width
    columns = lax.broadcasted_iota(jnp.int32, (rows, extra), 1)
    combine = jnp.zeros((rows, extra), jnp.float32)
    for k in range(routes_ref.shape[0]):
        route = jnp.concatenate([routes_ref[k : k + 1, r : r + 1] for r in range(rows)], axis=0)
        weight = weights_ref[:, k : k + 1].astype(jnp.float32)
        combine += jnp.where(columns == route, weight, 0.0)
    combine = combine.astype(jnp.bfloat16)
    for c in range(copies):
        packed_ref[c, :, :width] = tokens_ref[...]
        packed_ref[c, :, width:] = combine


def spacer_kernel(packed_ref, spare_hbm, mark_ref):
    mark_ref[...] = jnp.zeros_like(mark_ref)


def reorder_matrix(devs, tok_rows):
    half = devs * tok_rows
    shape = (2 * half, 2 * half)
    place = lax.broadcasted_iota(jnp.int32, shape, 0)
    source = lax.broadcasted_iota(jnp.int32, shape, 1)
    node = lax.axis_index("node")
    core = jnp.where(place < half, node, 1 - node)
    wanted = jnp.zeros(shape, jnp.int32)
    for c in range(2):
        for q in range(devs):
            held = SEND_ORDERS[c].index(RETURN_ORDERS[c][q])
            here = (core == c) & (place % half // tok_rows == q)
            wanted = jnp.where(here, held * tok_rows, wanted)
    wanted += place // half * half + place % tok_rows
    return (source == wanted).astype(jnp.bfloat16)


def expert_kernel(own_ref, other_ref, gate_ref, up_ref, down_ref, mark_ref, own_out, other_out):
    devs, tok_rows, wide = own_ref.shape
    _, width, hidden_units = gate_ref.shape
    rows = devs * tok_rows

    def tokens_part(part):
        halves = [ref[:, :, part] for ref in (own_ref, other_ref)]
        return jnp.concatenate([half.reshape(rows, half.shape[2]) for half in halves], axis=0)

    expert = lax.axis_index("node") * (lax.axis_size("dev") // SPLIT) + lax.axis_index("dev") // SPLIT
    combine = tokens_part(slice(width, wide))
    if devs == len(SEND_ORDERS[0]):
        reorder = reorder_matrix(devs, tok_rows)
        combine = jnp.dot(reorder, combine, preferred_element_type=jnp.float32)
    combine = combine.astype(jnp.float32)
    columns = lax.broadcasted_iota(jnp.int32, combine.shape, 1)
    scale = jnp.sum(jnp.where(columns == expert, combine, 0.0), axis=1, keepdims=True)
    gate = jnp.zeros((2 * rows, hidden_units), jnp.float32)
    upper = jnp.zeros((2 * rows, hidden_units), jnp.float32)
    for start in range(0, width, COLUMNS):
        part = slice(start, start + COLUMNS)
        block = tokens_part(part)
        gate += jnp.dot(block, gate_ref[0, part, :], preferred_element_type=jnp.float32)
        upper += jnp.dot(block, up_ref[0, part, :], preferred_element_type=jnp.float32)
    hidden = (gate / (1.0 + jnp.exp(-gate)) * upper).astype(jnp.bfloat16)
    if devs == len(SEND_ORDERS[0]):
        hidden = jnp.dot(reorder, hidden, preferred_element_type=jnp.float32).astype(jnp.bfloat16)
    for start in range(0, width, COLUMNS):
        part = slice(start, start + COLUMNS)
        output = scale * jnp.dot(
            hidden, down_ref[0, :, part], preferred_element_type=jnp.float32
        )
        own_out[:, part] = output[:rows]
        other_out[:, part] = output[rows:].astype(jnp.bfloat16)


def per_device(tokens, routes, route_weights, gate_weight, up_weight, down_weight):
    tok_rows, width = tokens.shape
    nodes = lax.axis_size("node")
    devs = lax.axis_size("dev")
    per_node = devs // SPLIT
    experts = nodes * per_node
    wide = width + -(-experts // LANES) * LANES
    vmem = pl.BlockSpec(memory_space=pltpu.VMEM)
    swap = [(i, i ^ 1) for i in range(nodes)]
    if devs == len(SEND_ORDERS[0]):
        orders = (SEND_ORDERS, RETURN_ORDERS)
    else:
        orders = ((tuple(range(devs)),) * nodes,) * 2
    send_groups, return_groups = (
        [[node * devs + dev for dev in order[node]] for node in range(nodes)] for order in orders
    )

    packed, spare = pl.pallas_call(
        pack_kernel,
        out_shape=(
            pltpu.VMEM((devs, tok_rows, wide), jnp.bfloat16),
            jax.ShapeDtypeStruct((SPARE, width), jnp.bfloat16),
        ),
        in_specs=[vmem] * 3,
        out_specs=(vmem, pl.BlockSpec(memory_space=pltpu.HBM)),
        name="pack",
    )(tokens, routes.T, route_weights)
    mark = pl.pallas_call(
        spacer_kernel,
        out_shape=pltpu.VMEM((8, LANES), jnp.float32),
        in_specs=[vmem, pl.BlockSpec(memory_space=pltpu.HBM)],
        out_specs=vmem,
        compiler_params=pltpu.CompilerParams(vmem_limit_bytes=SPACER_LIMIT),
        name="spacer",
    )(packed, spare)
    packed, mark = lax.optimization_barrier((packed, mark))
    own = lax.all_to_all(
        packed, ("node", "dev"), split_axis=0, concat_axis=0, tiled=True,
        axis_index_groups=send_groups,
    )
    other = lax.ppermute(own, "node", swap)
    own_out, other_out = pl.pallas_call(
        expert_kernel,
        out_shape=(
            jax.ShapeDtypeStruct((devs * tok_rows, width), jnp.float32),
            jax.ShapeDtypeStruct((devs * tok_rows, width), jnp.bfloat16),
        ),
        in_specs=[vmem] * 6,
        out_specs=(vmem, vmem),
        compiler_params=pltpu.CompilerParams(vmem_limit_bytes=VMEM_LIMIT),
        name="expert",
    )(own, other, gate_weight, up_weight, down_weight, mark)
    arrived = lax.ppermute(other_out, "node", swap)
    partial = (own_out + arrived.astype(jnp.float32)).astype(jnp.bfloat16)
    partial = partial.reshape(devs, tok_rows, width)
    returned = lax.all_to_all(
        partial, ("node", "dev"), split_axis=0, concat_axis=0, tiled=True,
        axis_index_groups=return_groups,
    )
    return jnp.sum(returned.astype(jnp.float32), axis=0).astype(jnp.bfloat16)


def solution(mesh):
    rows = P(("replica", "node", "dev"), None)
    shards = P(("node", "dev"), None, None)
    return jax.shard_map(
        per_device,
        mesh=mesh,
        in_specs=(rows, rows, rows, shards, shards, shards),
        out_specs=rows,
        check_vma=False,
    )
```

```python
import jax
import jax.numpy as jnp
from jax import lax
from jax.experimental import pallas as pl
from jax.experimental.pallas import tpu as pltpu
from jax.sharding import PartitionSpec as P

SPLIT = 8
LANES = 128
VMEM_LIMIT = 32 * 1024 * 1024
SPARE = 2048
SPACER_LIMIT = 38 * 1024 * 1024
COLUMNS = 1024
SEND_ORDERS = ((5, 7, 4, 0, 3, 1, 2, 6), (5, 6, 0, 2, 4, 3, 7, 1))
RETURN_ORDERS = ((5, 4, 3, 0, 7, 6, 1, 2), (4, 0, 3, 7, 1, 6, 5, 2))


def pack_kernel(tokens_ref, routes_ref, weights_ref, packed_ref, spare_ref):
    rows, width = tokens_ref.shape
    copies = packed_ref.shape[0]
    extra = packed_ref.shape[2] - width
    columns = lax.broadcasted_iota(jnp.int32, (rows, extra), 1)
    combine = jnp.zeros((rows, extra), jnp.float32)
    for k in range(routes_ref.shape[0]):
        route = jnp.concatenate([routes_ref[k : k + 1, r : r + 1] for r in range(rows)], axis=0)
        weight = weights_ref[:, k : k + 1].astype(jnp.float32)
        combine += jnp.where(columns == route, weight, 0.0)
    combine = combine.astype(jnp.bfloat16)
    for c in range(copies):
        packed_ref[c, :, :width] = tokens_ref[...]
        packed_ref[c, :, width:] = combine


def spacer_kernel(packed_ref, spare_hbm, mark_ref):
    mark_ref[...] = jnp.zeros_like(mark_ref)


def reorder_matrix(devs, tok_rows):
    half = devs * tok_rows
    shape = (2 * half, 2 * half)
    place = lax.broadcasted_iota(jnp.int32, shape, 0)
    source = lax.broadcasted_iota(jnp.int32, shape, 1)
    node = lax.axis_index("node")
    core = jnp.where(place < half, node, 1 - node)
    wanted = jnp.zeros(shape, jnp.int32)
    for c in range(2):
        for q in range(devs):
            held = SEND_ORDERS[c].index(RETURN_ORDERS[c][q])
            here = (core == c) & (place % half // tok_rows == q)
            wanted = jnp.where(here, held * tok_rows, wanted)
    wanted += place // half * half + place % tok_rows
    return (source == wanted).astype(jnp.bfloat16)


def expert_kernel(own_ref, other_ref, gate_ref, up_ref, down_ref, mark_ref, own_out, other_out):
    devs, tok_rows, wide = own_ref.shape
    _, width, hidden_units = gate_ref.shape
    rows = devs * tok_rows

    def tokens_part(part):
        halves = [ref[:, :, part] for ref in (own_ref, other_ref)]
        return jnp.concatenate([half.reshape(rows, half.shape[2]) for half in halves], axis=0)

    expert = lax.axis_index("node") * (lax.axis_size("dev") // SPLIT) + lax.axis_index("dev") // SPLIT
    combine = tokens_part(slice(width, wide))
    if devs == len(SEND_ORDERS[0]):
        reorder = reorder_matrix(devs, tok_rows)
        combine = jnp.dot(reorder, combine, preferred_element_type=jnp.float32)
    combine = combine.astype(jnp.float32)
    columns = lax.broadcasted_iota(jnp.int32, combine.shape, 1)
    scale = jnp.sum(jnp.where(columns == expert, combine, 0.0), axis=1, keepdims=True)
    gate = jnp.zeros((2 * rows, hidden_units), jnp.float32)
    upper = jnp.zeros((2 * rows, hidden_units), jnp.float32)
    for start in range(0, width, COLUMNS):
        part = slice(start, start + COLUMNS)
        block = tokens_part(part)
        gate += jnp.dot(block, gate_ref[0, part, :], preferred_element_type=jnp.float32)
        upper += jnp.dot(block, up_ref[0, part, :], preferred_element_type=jnp.float32)
    hidden = (gate / (1.0 + jnp.exp(-gate)) * upper).astype(jnp.bfloat16)
    if devs == len(SEND_ORDERS[0]):
        hidden = jnp.dot(reorder, hidden, preferred_element_type=jnp.float32).astype(jnp.bfloat16)
    for start in range(0, width, COLUMNS):
        part = slice(start, start + COLUMNS)
        output = scale * jnp.dot(
            hidden, down_ref[0, :, part], preferred_element_type=jnp.float32
        )
        own_out[:, part] = output[:rows]
        other_out[:, part] = output[rows:].astype(jnp.bfloat16)


def per_device(tokens, routes, route_weights, gate_weight, up_weight, down_weight):
    tok_rows, width = tokens.shape
    nodes = lax.axis_size("node")
    devs = lax.axis_size("dev")
    per_node = devs // SPLIT
    experts = nodes * per_node
    wide = width + -(-experts // LANES) * LANES
    vmem = pl.BlockSpec(memory_space=pltpu.VMEM)
    swap = [(i, i ^ 1) for i in range(nodes)]
    if devs == len(SEND_ORDERS[0]):
        orders = (SEND_ORDERS, RETURN_ORDERS)
    else:
        orders = ((tuple(range(devs)),) * nodes,) * 2
    send_groups, return_groups = (
        [[node * devs + dev for dev in order[node]] for node in range(nodes)] for order in orders
    )

    packed, spare = pl.pallas_call(
        pack_kernel,
        out_shape=(
            pltpu.VMEM((devs, tok_rows, wide), jnp.bfloat16),
            jax.ShapeDtypeStruct((SPARE, width), jnp.bfloat16),
        ),
        in_specs=[vmem] * 3,
        out_specs=(vmem, pl.BlockSpec(memory_space=pltpu.HBM)),
        name="pack",
    )(tokens, routes.T, route_weights)
    mark = pl.pallas_call(
        spacer_kernel,
        out_shape=pltpu.VMEM((8, LANES), jnp.float32),
        in_specs=[vmem, pl.BlockSpec(memory_space=pltpu.HBM)],
        out_specs=vmem,
        compiler_params=pltpu.CompilerParams(vmem_limit_bytes=SPACER_LIMIT),
        name="spacer",
    )(packed, spare)
    packed, mark = lax.optimization_barrier((packed, mark))
    own = lax.all_to_all(
        packed, ("node", "dev"), split_axis=0, concat_axis=0, tiled=True,
        axis_index_groups=send_groups,
    )
    other = lax.ppermute(own, "node", swap)
    own_out, other_out = pl.pallas_call(
        expert_kernel,
        out_shape=(
            jax.ShapeDtypeStruct((devs * tok_rows, width), jnp.float32),
            jax.ShapeDtypeStruct((devs * tok_rows, width), jnp.bfloat16),
        ),
        in_specs=[vmem] * 6,
        out_specs=(vmem, vmem),
        compiler_params=pltpu.CompilerParams(vmem_limit_bytes=VMEM_LIMIT),
        name="expert",
    )(own, other, gate_weight, up_weight, down_weight, mark)
    arrived = lax.ppermute(other_out, "node", swap)
    partial = (own_out + arrived.astype(jnp.float32)).astype(jnp.bfloat16)
    partial = partial.reshape(devs, tok_rows, width)
    returned = lax.all_to_all(
        partial, ("node", "dev"), split_axis=0, concat_axis=0, tiled=True,
        axis_index_groups=return_groups,
    )
    return jnp.sum(returned.astype(jnp.float32), axis=0).astype(jnp.bfloat16)


def solution(mesh):
    rows = P(("replica", "node", "dev"), None)
    shards = P(("node", "dev"), None, None)
    return jax.shard_map(
        per_device,
        mesh=mesh,
        in_specs=(rows, rows, rows, shards, shards, shards),
        out_specs=rows,
        check_vma=False,
    )
```
